32 devices in a mesh: groups: 2 (over x), expert: 4 (over y, core), dp: 4 (over z).
Axes of the slice: x: 2, y: 2, z: 4, core: 2. Of those that a mesh axis runs over, the one named last changes fastest.
Arguments:
- tokens: bfloat16 [4096, 7168], P(('groups', 'expert', 'dp')), parts along dimension 0, may hold values from -6 to 6
- cotangent: bfloat16 [4096, 7168], P(('groups', 'expert', 'dp')), parts along dimension 0, may hold values from -1.1953125 to 1.1953125
- route_ids: int32 [4096, 8], P(('groups', 'expert', 'dp')), parts along dimension 0, may hold values from 0 to 255, as said below
- route_weight: bfloat16 [4096, 8], P(('groups', 'expert', 'dp')), parts along dimension 0, may hold values from 0.049804688 to 0.5
- gate_weight: bfloat16 [4, 7168, 1024], P('expert', None, 'dp'), may hold values from -0.0625 to 0.0625
- up_weight: bfloat16 [4, 7168, 1024], P('expert', None, 'dp'), may hold values from -0.0625 to 0.0625
- down_weight: bfloat16 [4, 1024, 7168], P('expert', 'dp'), may hold values from -0.0625 to 0.0625
Outputs:
- grad_gate: bfloat16 [8, 7168, 1024], P(('groups', 'expert'), None, 'dp'), parts along dimension 0
- grad_up: bfloat16 [8, 7168, 1024], P(('groups', 'expert'), None, 'dp'), parts along dimension 0
- route_grad: float32 [4096, 8], P(('groups', 'expert', 'dp')), parts along dimension 0
The draws below stay inside these ranges and needn't reach their ends.
There are 2 independent parts, one for each index of `groups`. The reference program is written for one: setup_inputs(seed, part) draws one part's arguments, and reference() takes and returns one part's arrays. A program takes and returns all parts, laid end to end along the dimension named above; an argument that names none is the same for every part. Nothing has to cross between parts.
Inputs may be any that keep to these rules, and one draw needn't show every extreme that they name: `route_ids`: each token names 8 different experts. Of the tokens of one device (aligned blocks of 128 rows), at most 8 name any one expert below 4, and one such expert is named by exactly 8 tokens of every device.
All inputs are finite; a program needn't handle non-finite values.
Results may differ from the reference program's by a relative error of at most 0.0049.
Values may be sent and summed in bfloat16 or wider, within the bound.
A program may use at most 128 MiB of HBM per device.

```python
import math
import jax
import jax.numpy as jnp
from jax import lax

D = 7168
FF = 1024
ALL_EXPERTS = 256
TOPK = 8
TOK_DEV = 128
EXPERTS = 4
CAP = 8
TOKENS = 2048
N_DP = 4


def draw_route_ids(key, part):
    id_span = ALL_EXPERTS // TOPK
    blocks = TOKENS // TOK_DEV
    key_list = jax.random.split(key, 5)
    hot_id = jax.random.randint(key_list[0], (), 0, EXPERTS)
    offsets = jax.random.randint(key_list[1], (blocks, 1), 0, id_span - 1)
    column = jnp.arange(TOK_DEV, dtype=jnp.int32)[None, :]
    others = (offsets + column) % (id_span - 1)
    others = jnp.where(others >= hot_id, others + 1, others)
    lead_ids = jnp.where(column < CAP, hot_id, others)
    shuffles = jax.vmap(lambda sub_key: jax.random.permutation(sub_key, TOK_DEV))(jax.random.split(key_list[2], blocks))
    lead_ids = jnp.take_along_axis(lead_ids, shuffles, axis=1).reshape(TOKENS)
    tail_ids = jax.random.randint(key_list[3], (TOKENS, TOPK - 1), 0, id_span) + id_span * jnp.arange(1, TOPK, dtype=jnp.int32)[None, :]
    chosen = jnp.concatenate([lead_ids[:, None], tail_ids], axis=1)
    orders = jax.vmap(lambda sub_key: jax.random.permutation(sub_key, TOPK))(jax.random.split(key_list[4], TOKENS))
    return jnp.take_along_axis(chosen, orders, axis=1).astype(jnp.int32)


def block_scale(key, extent, pieces, least, high):
    gain, own = 1.0, jax.random.fold_in(key, 6)
    for dim, parts in pieces:
        steps = jnp.exp(jax.random.uniform(jax.random.fold_in(own, dim), (parts,), jnp.float32, least / len(pieces), high / len(pieces)))
        gain = gain * jnp.repeat(steps, extent[dim] // parts).reshape([-1 if axis == dim else 1 for axis in range(len(extent))])
    return gain


def normal_values(own_key, extent, scale, most, shards=(), kind=jnp.bfloat16):
    result = jax.random.normal(own_key, extent, jnp.float32) * scale
    if len(shards) > 0:
        result = block_scale(own_key, extent, shards, -0.22, 0.18) * result
    return jnp.clip(result, min=-most, max=most).astype(kind)


def setup_inputs(seed: int = 0, part: int = 0) -> dict:
    key_of = jax.random.split(jax.random.key(seed), 8)
    own_keys = jax.random.split(jax.random.fold_in(key_of[7], part), 8)
    tokens = normal_values(own_keys[0], (TOKENS, D), 1.0, 6.0, ((0, 16),))
    cotangent = normal_values(own_keys[1], (TOKENS, D), 0.2, 1.1953125, ((0, 16),))
    route_ids = draw_route_ids(jax.random.fold_in(jax.random.fold_in(key_of[7], part), 71), part)
    route_weight = jnp.clip(jnp.exp(math.log(0.5) - 2.306499 * jax.random.uniform(own_keys[3], (TOKENS, TOPK), jnp.float32) ** block_scale(own_keys[3], (TOKENS, TOPK), ((0, 16),), -0.2, 0.2)), 0.049804688, 0.5).astype(jnp.bfloat16)
    gate_weight = normal_values(key_of[4], (EXPERTS, D, FF), D ** -0.5, 0.0625, ((0, 4), (2, 4)))
    up_weight = normal_values(key_of[5], (EXPERTS, D, FF), D ** -0.5, 0.0625, ((0, 4), (2, 4)))
    down_weight = normal_values(key_of[6], (EXPERTS, FF, D), D ** -0.5, 0.0625, ((0, 4), (1, 4)))
    return {"tokens": tokens, "cotangent": cotangent, "route_ids": route_ids, "route_weight": route_weight, "gate_weight": gate_weight, "up_weight": up_weight, "down_weight": down_weight}


def reference(tokens, cotangent, route_ids, route_weight, gate_weight, up_weight, down_weight):
    most_rows = EXPERTS * N_DP * CAP

    def one_expert(expert_id):
        chosen = route_ids == expert_id
        picked = jnp.any(chosen, axis=1)
        weight_tok = jnp.sum(jnp.where(chosen, route_weight.astype(jnp.float32), 0.0), axis=1)
        row_order = jnp.argsort(jnp.where(picked, 0, 1).astype(jnp.int32), stable=True)[:most_rows]
        live_rows = picked[row_order].astype(jnp.float32)
        row_block = tokens[row_order]
        cot_block = cotangent[row_order]
        gate_pre = jnp.dot(row_block, gate_weight[expert_id], preferred_element_type=jnp.float32)
        up_pre = jnp.dot(row_block, up_weight[expert_id], preferred_element_type=jnp.float32)
        back_proj = jnp.dot(cot_block, down_weight[expert_id].T, preferred_element_type=jnp.float32)
        gate_sig = jax.nn.sigmoid(gate_pre)
        gate_act = gate_pre * gate_sig
        slot_sum = jnp.sum(gate_act * up_pre * back_proj, axis=1) * live_rows
        act_grad = (weight_tok[row_order] * live_rows)[:, None] * back_proj
        d_gate = (act_grad * up_pre * gate_sig * (1.0 + gate_pre * (1.0 - gate_sig))).astype(jnp.bfloat16)
        d_up = (act_grad * gate_act).astype(jnp.bfloat16)
        grad_g = jnp.dot(row_block.T, d_gate, preferred_element_type=jnp.float32).astype(jnp.bfloat16)
        grad_u = jnp.dot(row_block.T, d_up, preferred_element_type=jnp.float32).astype(jnp.bfloat16)
        tok_sum = jnp.zeros((TOKENS,), jnp.float32).at[row_order].add(slot_sum)
        slot_grad = jnp.where(chosen, tok_sum[:, None], jnp.zeros((), jnp.float32))
        return grad_g, grad_u, slot_grad

    grad_gate, grad_up, slot_grads = lax.map(one_expert, jnp.arange(EXPERTS, dtype=jnp.int32))
    return grad_gate, grad_up, jnp.sum(slot_grads, axis=0)
```

```python
import jax
import jax.numpy as jnp
from jax import lax
from jax.sharding import PartitionSpec as P

CAP = 8


def dot_first(a, b):
    return lax.dot_general(a, b, (((0,), (0,)), ((), ())), preferred_element_type=jnp.float32)


def general(tokens, cotangent, route_ids, route_weight, gate_weight, up_weight, down_weight):
    expert_count = lax.axis_size("expert")
    dp_count = lax.axis_size("dp")
    tok_count, model_width = tokens.shape
    experts = jnp.arange(expert_count, dtype=jnp.int32)
    hit = route_ids[:, :, None] == experts[None, None, :]
    chosen = jnp.any(hit, axis=1)
    weight_tok = jnp.sum(jnp.where(hit, route_weight.astype(jnp.float32)[:, :, None], 0.0), axis=1)
    row = jnp.arange(tok_count, dtype=jnp.int32)
    earlier = (row[None, :] < row[:, None]).astype(jnp.bfloat16)
    rank = jnp.dot(earlier, chosen.astype(jnp.bfloat16), preferred_element_type=jnp.float32).astype(jnp.int32)
    place = jnp.arange(CAP, dtype=jnp.int32)
    select = chosen[:, :, None] & (rank[:, :, None] == place[None, None, :])
    onehot = select.reshape(tok_count, expert_count * CAP).astype(jnp.bfloat16)
    send_weight = jnp.sum(jnp.where(select, weight_tok[:, :, None], 0.0), axis=0).astype(jnp.bfloat16)
    send_rows = dot_first(onehot, tokens).astype(jnp.bfloat16).reshape(expert_count, CAP, model_width)
    send_cots = dot_first(onehot, cotangent).astype(jnp.bfloat16).reshape(expert_count, CAP, model_width)

    def widen_rows(array):
        spread = jnp.broadcast_to(array[:, None], (expert_count, dp_count) + array.shape[1:])
        return spread.reshape((expert_count * dp_count,) + array.shape[1:])

    def exchange(array):
        return lax.all_to_all(array, ("expert", "dp"), split_axis=0, concat_axis=0, tiled=True)

    row_block = exchange(widen_rows(send_rows)).reshape(-1, model_width)
    cot_block = exchange(widen_rows(send_cots)).reshape(-1, model_width)
    weights = exchange(widen_rows(send_weight)).reshape(-1).astype(jnp.float32)
    gate_pre = jnp.dot(row_block, gate_weight[0], preferred_element_type=jnp.float32)
    up_pre = jnp.dot(row_block, up_weight[0], preferred_element_type=jnp.float32)
    back_proj = lax.dot_general(
        cot_block, down_weight[0], (((1,), (1,)), ((), ())), preferred_element_type=jnp.float32
    )
    gate_sig = jax.nn.sigmoid(gate_pre)
    gate_act = gate_pre * gate_sig
    partial = jnp.sum(gate_act * up_pre * back_proj, axis=1).reshape(expert_count * dp_count, CAP)
    act_grad = weights[:, None] * back_proj
    d_gate = (act_grad * up_pre * gate_sig * (1.0 + gate_pre * (1.0 - gate_sig))).astype(jnp.bfloat16)
    d_up = (act_grad * gate_act).astype(jnp.bfloat16)
    grad_gate = dot_first(row_block, d_gate).astype(jnp.bfloat16)
    grad_up = dot_first(row_block, d_up).astype(jnp.bfloat16)
    returned = exchange(partial)
    slot_sums = jnp.sum(returned.reshape(expert_count, dp_count, CAP), axis=1)
    value = jnp.sum(jnp.where(select, slot_sums[None], 0.0), axis=2)
    route_grad = jnp.sum(jnp.where(hit, value[:, None, :], 0.0), axis=2)
    return grad_gate[None], grad_up[None], route_grad


def solution(mesh):
    return jax.shard_map(
        general,
        mesh=mesh,
        in_specs=(
            P(("groups", "expert", "dp"), None),
            P(("groups", "expert", "dp"), None),
            P(("groups", "expert", "dp"), None),
            P(("groups", "expert", "dp"), None),
            P("expert", None, "dp"),
            P("expert", None, "dp"),
            P("expert", "dp", None),
        ),
        out_specs=(
            P(("groups", "expert"), None, "dp"),
            P(("groups", "expert"), None, "dp"),
            P(("groups", "expert", "dp"), None),
        ),
        check_vma=False,
    )
```

```python
import functools
import math

import jax
import jax.numpy as jnp
from jax import lax
from jax.experimental import pallas as pl
from jax.experimental.pallas import tpu as pltpu
from jax.sharding import PartitionSpec as P

CAP = 8


def dot_first(a, b):
    return lax.dot_general(a, b, (((0,), (0,)), ((), ())), preferred_element_type=jnp.float32)


def general(tokens, cotangent, route_ids, route_weight, gate_weight, up_weight, down_weight):
    expert_count = lax.axis_size("expert")
    dp_count = lax.axis_size("dp")
    tok_count, model_width = tokens.shape
    experts = jnp.arange(expert_count, dtype=jnp.int32)
    hit = route_ids[:, :, None] == experts[None, None, :]
    chosen = jnp.any(hit, axis=1)
    weight_tok = jnp.sum(jnp.where(hit, route_weight.astype(jnp.float32)[:, :, None], 0.0), axis=1)
    row = jnp.arange(tok_count, dtype=jnp.int32)
    earlier = (row[None, :] < row[:, None]).astype(jnp.bfloat16)
    rank = jnp.dot(earlier, chosen.astype(jnp.bfloat16), preferred_element_type=jnp.float32).astype(jnp.int32)
    place = jnp.arange(CAP, dtype=jnp.int32)
    select = chosen[:, :, None] & (rank[:, :, None] == place[None, None, :])
    onehot = select.reshape(tok_count, expert_count * CAP).astype(jnp.bfloat16)
    send_weight = jnp.sum(jnp.where(select, weight_tok[:, :, None], 0.0), axis=0).astype(jnp.bfloat16)
    send_rows = dot_first(onehot, tokens).astype(jnp.bfloat16).reshape(expert_count, CAP, model_width)
    send_cots = dot_first(onehot, cotangent).astype(jnp.bfloat16).reshape(expert_count, CAP, model_width)

    def widen_rows(array):
        spread = jnp.broadcast_to(array[:, None], (expert_count, dp_count) + array.shape[1:])
        return spread.reshape((expert_count * dp_count,) + array.shape[1:])

    def exchange(array):
        return lax.all_to_all(array, ("expert", "dp"), split_axis=0, concat_axis=0, tiled=True)

    row_block = exchange(widen_rows(send_rows)).reshape(-1, model_width)
    cot_block = exchange(widen_rows(send_cots)).reshape(-1, model_width)
    weights = exchange(widen_rows(send_weight)).reshape(-1).astype(jnp.float32)
    gate_pre = jnp.dot(row_block, gate_weight[0], preferred_element_type=jnp.float32)
    up_pre = jnp.dot(row_block, up_weight[0], preferred_element_type=jnp.float32)
    back_proj = lax.dot_general(
        cot_block, down_weight[0], (((1,), (1,)), ((), ())), preferred_element_type=jnp.float32
    )
    gate_sig = jax.nn.sigmoid(gate_pre)
    gate_act = gate_pre * gate_sig
    partial = jnp.sum(gate_act * up_pre * back_proj, axis=1).reshape(expert_count * dp_count, CAP)
    act_grad = weights[:, None] * back_proj
    d_gate = (act_grad * up_pre * gate_sig * (1.0 + gate_pre * (1.0 - gate_sig))).astype(jnp.bfloat16)
    d_up = (act_grad * gate_act).astype(jnp.bfloat16)
    grad_gate = dot_first(row_block, d_gate).astype(jnp.bfloat16)
    grad_up = dot_first(row_block, d_up).astype(jnp.bfloat16)
    returned = exchange(partial)
    slot_sums = jnp.sum(returned.reshape(expert_count, dp_count, CAP), axis=1)
    value = jnp.sum(jnp.where(select, slot_sums[None], 0.0), axis=2)
    route_grad = jnp.sum(jnp.where(hit, value[:, None, :], 0.0), axis=2)
    return grad_gate[None], grad_up[None], route_grad


PAIR = 2


def move_kernel(
    shape, ids_ref, rw_ref, tok_hbm, cot_hbm, wg_hbm, wu_hbm, wd_hbm,
    rows_ref, dcat_ref, grad_ref,
    cots_ref, tok_ref, cot_ref, wg_ref, wu_ref, wd_ref, st_ref, sc_ref, pbuf, rbuf,
    load_sem, y_sem, up_sem, down_sem, core_sem, recv_sem, back_sem, home_sem,
):
    y_count, z_count, cap = shape
    width = tok_ref.shape[1]
    hidden = wg_ref.shape[1]
    toks = tok_ref.shape[0]
    chunk = math.gcd(width, 1024)
    me = lax.axis_index("expert")
    z = lax.axis_index("dp")
    y, c = lax.div(me, PAIR), lax.rem(me, PAIR)
    slots = y_count * cap
    plane = PAIR * slots

    loads = [
        pltpu.make_async_copy(src, dst, load_sem.at[i])
        for i, (src, dst) in enumerate(
            ((tok_hbm, tok_ref), (cot_hbm, cot_ref), (wg_hbm, wg_ref), (wu_hbm, wu_ref), (wd_hbm, wd_ref))
        )
    ]
    for load in loads:
        load.start()

    group = PAIR * y_count * z_count
    mine = me * z_count + z

    def place_of(index):
        return {"expert": lax.div(index, z_count), "dp": lax.rem(index, z_count)}

    barrier = pltpu.get_barrier_semaphore()
    for step in range(1, group):
        pl.semaphore_signal(
            barrier, inc=1, device_id=place_of(lax.rem(mine + step, group)), device_id_type=pl.DeviceIdType.MESH
        )

    ids = ids_ref[...]
    rw = rw_ref[...].astype(jnp.float32)
    experts = PAIR * y_count
    padded = -(-experts // 16) * 16
    number = lax.broadcasted_iota(jnp.int32, (padded, toks), 0)
    chosen = jnp.zeros((padded, toks), jnp.float32)
    for k in range(ids.shape[0]):
        chosen += jnp.where(ids[k : k + 1, :] == number, 1.0, 0.0)
    earlier = lax.broadcasted_iota(jnp.int32, (toks, toks), 0) < lax.broadcasted_iota(jnp.int32, (toks, toks), 1)
    upper = jnp.where(earlier, 1.0, 0.0).astype(jnp.bfloat16)
    rank = jnp.dot(chosen.astype(jnp.bfloat16), upper, preferred_element_type=jnp.float32)
    total = jnp.sum(chosen, axis=1, keepdims=True)
    slot = lax.broadcasted_iota(jnp.int32, (slots, toks), 0).astype(jnp.float32)
    lane = lax.broadcasted_iota(jnp.int32, (slots, 128), 1)
    select = jnp.zeros((slots, toks), jnp.float32)
    tail = jnp.zeros((slots, 128), jnp.float32)
    picks = []
    for e in range(experts):
        spot = rank[e : e + 1, :] + float((e // PAIR) * cap)
        if e % PAIR:
            spot = spot + total[e - 1 : e, :]
        pick = jnp.where((slot == spot) & (chosen[e : e + 1, :] > 0.5), 1.0, 0.0)
        weight = jnp.sum(jnp.where(ids == e, rw, 0.0), axis=0, keepdims=True)
        tail += jnp.where(lane == e % PAIR, jnp.sum(pick * weight, axis=1, keepdims=True), 0.0)
        select += pick
        picks.append(pick)
    select = select.astype(jnp.bfloat16)

    def row_of(z_src, c_src, y_src):
        return pl.multiple_of(((z_src * PAIR + c_src) * y_count + y_src) * cap, cap)

    def block(kind, z_src, c_src, y_src):
        ref = rows_ref if kind == 0 else cots_ref
        return ref.at[pl.ds(row_of(z_src, c_src, y_src), cap), :]

    def remote(kind, z_src, c_src, y_src, send_sem, target, src=None):
        there = block(kind, z_src, c_src, y_src)
        return pltpu.make_async_remote_copy(
            src_ref=there if src is None else src,
            dst_ref=there,
            send_sem=send_sem,
            recv_sem=recv_sem.at[z_src, c_src, y_src, kind],
            device_id=target,
            device_id_type=pl.DeviceIdType.MESH,
        )

    def to_up(kind, z_src, y_src):
        return remote(kind, z_src, c, y_src, up_sem.at[z_src, y_src, kind], {"dp": z + 1})

    def to_down(kind, z_src, y_src):
        return remote(kind, z_src, c, y_src, down_sem.at[z_src, y_src, kind], {"dp": z - 1})

    def to_core(kind, z_src, y_src):
        return remote(kind, z_src, c, y_src, core_sem.at[z_src, y_src, kind], {"expert": y * PAIR + 1 - c})

    def to_y(kind, step):
        y_to = lax.rem(y + step, y_count)
        ref = st_ref if kind == 0 else sc_ref
        src = ref.at[pl.ds(pl.multiple_of(y_to * cap, cap), cap), :]
        return remote(kind, z, c, y, y_sem.at[step, kind], {"expert": y_to * PAIR + c}, src)

    def arrived(kind, z_src, c_src, y_src):
        there = block(kind, z_src, c_src, y_src)
        pltpu.make_async_remote_copy(
            src_ref=there, dst_ref=there, send_sem=load_sem.at[0], recv_sem=recv_sem.at[z_src, c_src, y_src, kind],
            device_id={"expert": y * PAIR + 1 - c}, device_id_type=pl.DeviceIdType.MESH,
        ).wait_recv()

    def spread(kind, y_src):
        @pl.when(z + 1 < z_count)
        def _():
            to_up(kind, z, y_src).start()

        @pl.when(z > 0)
        def _():
            to_down(kind, z, y_src).start()

        to_core(kind, z, y_src).start()

    own = pl.ds(pl.multiple_of(y * cap, cap), cap)
    for kind, (load, src, out) in enumerate(((loads[0], tok_ref, st_ref), (loads[1], cot_ref, sc_ref))):
        load.wait()

        @pl.loop(0, width // chunk)
        def _(i, src=src, out=out):
            at = pl.ds(pl.multiple_of(i * chunk, chunk), chunk)
            out[:, at] = jnp.dot(select, src[:, at], preferred_element_type=jnp.float32).astype(jnp.bfloat16)

        if kind == 0:
            st_ref[:, width:] = tail.astype(jnp.bfloat16)
            pl.semaphore_wait(barrier, group - 1)
        for step in range(1, y_count):
            to_y(kind, step).start()
        (rows_ref if kind == 0 else cots_ref)[pl.ds(row_of(z, c, y), cap), :] = out[own, :]
        spread(kind, y)
    for kind in range(2):
        for step in range(1, y_count):
            y_src = lax.rem(y + y_count - step, y_count)
            arrived(kind, z, c, y_src)
            spread(kind, y_src)

    def forward(z_src):
        for kind in range(2):
            for y_src in range(y_count):
                arrived(kind, z_src, 1 - c, y_src)
        rows = pl.ds(pl.multiple_of(z_src * plane, plane), plane)

        def add(i, sums):
            at = pl.ds(pl.multiple_of(i * chunk, chunk), chunk)
            x, t = rows_ref[rows, at], cots_ref[rows, at]
            return (
                sums[0] + jnp.dot(x, wg_ref[at, :], preferred_element_type=jnp.float32),
                sums[1] + jnp.dot(x, wu_ref[at, :], preferred_element_type=jnp.float32),
                sums[2]
                + lax.dot_general(t, wd_ref[:, at], (((1,), (1,)), ((), ())), preferred_element_type=jnp.float32),
            )

        zero = jnp.zeros((plane, hidden), jnp.float32)
        gate_pre, up_pre, back = lax.fori_loop(0, width // chunk, add, (zero, zero, zero))
        sig = jax.nn.sigmoid(gate_pre)
        act = gate_pre * sig
        part = jnp.sum(act * up_pre * back, axis=1, keepdims=True)
        pbuf[rows, :] = jnp.broadcast_to(part, (plane, 128))
        marks = rows_ref[rows, width:].astype(jnp.float32)
        which = lax.broadcasted_iota(jnp.int32, (plane, 128), 1)
        weight = jnp.sum(jnp.where(which == c, marks, 0.0), axis=1, keepdims=True)
        act_grad = weight * back
        dcat_ref[rows, :hidden] = (act_grad * up_pre * sig * (1.0 + gate_pre * (1.0 - sig))).astype(jnp.bfloat16)
        dcat_ref[rows, hidden:] = (act_grad * act).astype(jnp.bfloat16)

    def home(z_to, c_to, y_to):
        return pltpu.make_async_remote_copy(
            src_ref=pbuf.at[pl.ds(row_of(z_to, c_to, y_to), cap), :],
            dst_ref=rbuf.at[pl.ds(pl.multiple_of(mine * cap, cap), cap), :],
            send_sem=back_sem.at[z_to, c_to, y_to],
            recv_sem=home_sem.at[mine],
            device_id={"expert": y_to * PAIR + c_to, "dp": z_to},
            device_id_type=pl.DeviceIdType.MESH,
        )

    def not_me(z_to, c_to, y_to):
        return (z_to != z) | (c_to != c) | (y_to != y)

    def go_home(z_to):
        for c_to in range(PAIR):
            for y_to in range(y_count):

                @pl.when(not_me(z_to, c_to, y_to))
                def _(c_to=c_to, y_to=y_to):
                    home(z_to, c_to, y_to).start()

    for load in loads[2:]:
        load.wait()
    for hop in range(1, z_count):
        for kind in range(2):
            for step in range(y_count):
                y_src = lax.rem(y + y_count - step, y_count)

                @pl.when(z >= hop)
                def _(kind=kind, y_src=y_src, hop=hop):
                    arrived(kind, z - hop, c, y_src)

                    @pl.when(z + 1 < z_count)
                    def _():
                        to_up(kind, z - hop, y_src).start()

                    to_core(kind, z - hop, y_src).start()

                @pl.when(z + hop < z_count)
                def _(kind=kind, y_src=y_src, hop=hop):
                    arrived(kind, z + hop, c, y_src)

                    @pl.when(z > 0)
                    def _():
                        to_down(kind, z + hop, y_src).start()

                    to_core(kind, z + hop, y_src).start()

            if kind == 0:
                if hop == 1:
                    forward(z)
                    go_home(z)
                else:

                    @pl.when(z >= hop - 1)
                    def _(hop=hop):
                        forward(z - (hop - 1))
                        go_home(z - (hop - 1))

                    @pl.when(z + hop - 1 < z_count)
                    def _(hop=hop):
                        forward(z + (hop - 1))
                        go_home(z + (hop - 1))

    last = z_count - 1
    if last == 0:
        forward(z)
        go_home(z)
    else:

        @pl.when(z >= last)
        def _():
            forward(z - last)
            go_home(z - last)

        @pl.when(z + last < z_count)
        def _():
            forward(z + last)
            go_home(z + last)

    rbuf[pl.ds(pl.multiple_of(mine * cap, cap), cap), :] = pbuf[pl.ds(row_of(z, c, y), cap), :]

    for kind in range(2):
        for step in range(1, y_count):
            to_y(kind, step).wait_send()
        for z_src in range(z_count):
            for y_src in range(y_count):
                to_core(kind, z_src, y_src).wait_send()

                @pl.when((z_src <= z) & (z + 1 < z_count))
                def _(kind=kind, z_src=z_src, y_src=y_src):
                    to_up(kind, z_src, y_src).wait_send()

                @pl.when((z_src >= z) & (z > 0))
                def _(kind=kind, z_src=z_src, y_src=y_src):
                    to_down(kind, z_src, y_src).wait_send()

    for z_to in range(z_count):
        for c_to in range(PAIR):
            for y_to in range(y_count):

                @pl.when(not_me(z_to, c_to, y_to))
                def _(z_to=z_to, c_to=c_to, y_to=y_to):
                    home(z_to, c_to, y_to).wait_send()
                    spot = (y_to * PAIR + c_to) * z_count + z_to
                    there = rbuf.at[pl.ds(spot * cap, cap), :]
                    pltpu.make_async_remote_copy(
                        src_ref=there, dst_ref=there, send_sem=load_sem.at[0], recv_sem=home_sem.at[spot],
                        device_id={"expert": y * PAIR + 1 - c}, device_id_type=pl.DeviceIdType.MESH,
                    ).wait_recv()

    result = jnp.zeros(ids.shape, jnp.float32)
    for e in range(experts):
        first = e * z_count * cap
        sums = rbuf[first : first + cap, :]
        for k in range(1, z_count):
            sums = sums + rbuf[first + k * cap : first + (k + 1) * cap, :]
        pick = picks[e][(e // PAIR) * cap : (e // PAIR + 1) * cap, :]
        value = jnp.sum(pick * sums, axis=0, keepdims=True)
        result += jnp.where(ids == e, value, 0.0)
    grad_ref[...] = result


def moved(tokens, cotangent, route_ids, route_weight, gate_weight, up_weight, down_weight):
    y_count = lax.axis_size("expert") // PAIR
    z_count = lax.axis_size("dp")
    cap = PAIR * CAP
    tok_count, width = tokens.shape
    hidden = gate_weight.shape[2]
    count = PAIR * y_count * z_count * cap
    dma = pltpu.SemaphoreType.DMA
    rows, dcat, grad = pl.pallas_call(
        functools.partial(move_kernel, (y_count, z_count, cap)),
        out_shape=(
            jax.ShapeDtypeStruct((count, width + 128), jnp.bfloat16),
            jax.ShapeDtypeStruct((count, 2 * hidden), jnp.bfloat16),
            jax.ShapeDtypeStruct(route_ids.shape[::-1], jnp.float32),
        ),
        in_specs=[pl.BlockSpec(memory_space=pltpu.VMEM)] * 2 + [pl.BlockSpec(memory_space=pl.ANY)] * 5,
        out_specs=[pl.BlockSpec(memory_space=pltpu.VMEM)] * 3,
        scratch_shapes=[
            pltpu.VMEM((count, width), jnp.bfloat16),
            pltpu.VMEM((tok_count, width), jnp.bfloat16),
            pltpu.VMEM((tok_count, width), jnp.bfloat16),
            pltpu.VMEM((width, hidden), jnp.bfloat16),
            pltpu.VMEM((width, hidden), jnp.bfloat16),
            pltpu.VMEM((hidden, width), jnp.bfloat16),
            pltpu.VMEM((y_count * cap, width + 128), jnp.bfloat16),
            pltpu.VMEM((y_count * cap, width), jnp.bfloat16),
            pltpu.VMEM((count, 128), jnp.float32),
            pltpu.VMEM((count, 128), jnp.float32),
            dma((5,)),
            dma((y_count, 2)),
            dma((z_count, y_count, 2)),
            dma((z_count, y_count, 2)),
            dma((z_count, y_count, 2)),
            dma((z_count, PAIR, y_count, 2)),
            dma((z_count, PAIR, y_count)),
            dma((PAIR * y_count * z_count,)),
        ],
        compiler_params=pltpu.CompilerParams(
            collective_id=0, has_side_effects=True, vmem_limit_bytes=48 * 2**20
        ),
        cost_estimate=pl.CostEstimate(
            flops=6 * count * width * hidden, bytes_accessed=8 * width * hidden, transcendentals=count * hidden
        ),
    )(route_ids.T, route_weight.T, tokens, cotangent, gate_weight[0], up_weight[0], down_weight[0])
    row_block = rows[:, :width]
    grad_gate = dot_first(row_block, dcat[:, :hidden]).astype(jnp.bfloat16)
    grad_up = dot_first(row_block, dcat[:, hidden:]).astype(jnp.bfloat16)
    return grad_gate[None], grad_up[None], grad.T


def fits(mesh):
    return mesh.shape["expert"] % PAIR == 0 and mesh.shape["expert"] * mesh.shape["dp"] <= 16


def solution(mesh):
    return jax.shard_map(
        moved if fits(mesh) else general,
        mesh=mesh,
        in_specs=(
            P(("groups", "expert", "dp"), None),
            P(("groups", "expert", "dp"), None),
            P(("groups", "expert", "dp"), None),
            P(("groups", "expert", "dp"), None),
            P("expert", None, "dp"),
            P("expert", None, "dp"),
            P("expert", "dp", None),
        ),
        out_specs=(
            P(("groups", "expert"), None, "dp"),
            P(("groups", "expert"), None, "dp"),
            P(("groups", "expert", "dp"), None),
        ),
        check_vma=False,
    )
```

```python
import functools
import math

import jax
import jax.numpy as jnp
from jax import lax
from jax.experimental import pallas as pl
from jax.experimental.pallas import tpu as pltpu
from jax.sharding import PartitionSpec as P

CAP = 8


def dot_first(a, b):
    return lax.dot_general(a, b, (((0,), (0,)), ((), ())), preferred_element_type=jnp.float32)


def general(tokens, cotangent, route_ids, route_weight, gate_weight, up_weight, down_weight):
    expert_count = lax.axis_size("expert")
    dp_count = lax.axis_size("dp")
    tok_count, model_width = tokens.shape
    experts = jnp.arange(expert_count, dtype=jnp.int32)
    hit = route_ids[:, :, None] == experts[None, None, :]
    chosen = jnp.any(hit, axis=1)
    weight_tok = jnp.sum(jnp.where(hit, route_weight.astype(jnp.float32)[:, :, None], 0.0), axis=1)
    row = jnp.arange(tok_count, dtype=jnp.int32)
    earlier = (row[None, :] < row[:, None]).astype(jnp.bfloat16)
    rank = jnp.dot(earlier, chosen.astype(jnp.bfloat16), preferred_element_type=jnp.float32).astype(jnp.int32)
    place = jnp.arange(CAP, dtype=jnp.int32)
    select = chosen[:, :, None] & (rank[:, :, None] == place[None, None, :])
    onehot = select.reshape(tok_count, expert_count * CAP).astype(jnp.bfloat16)
    send_weight = jnp.sum(jnp.where(select, weight_tok[:, :, None], 0.0), axis=0).astype(jnp.bfloat16)
    send_rows = dot_first(onehot, tokens).astype(jnp.bfloat16).reshape(expert_count, CAP, model_width)
    send_cots = dot_first(onehot, cotangent).astype(jnp.bfloat16).reshape(expert_count, CAP, model_width)

    def widen_rows(array):
        spread = jnp.broadcast_to(array[:, None], (expert_count, dp_count) + array.shape[1:])
        return spread.reshape((expert_count * dp_count,) + array.shape[1:])

    def exchange(array):
        return lax.all_to_all(array, ("expert", "dp"), split_axis=0, concat_axis=0, tiled=True)

    row_block = exchange(widen_rows(send_rows)).reshape(-1, model_width)
    cot_block = exchange(widen_rows(send_cots)).reshape(-1, model_width)
    weights = exchange(widen_rows(send_weight)).reshape(-1).astype(jnp.float32)
    gate_pre = jnp.dot(row_block, gate_weight[0], preferred_element_type=jnp.float32)
    up_pre = jnp.dot(row_block, up_weight[0], preferred_element_type=jnp.float32)
    back_proj = lax.dot_general(
        cot_block, down_weight[0], (((1,), (1,)), ((), ())), preferred_element_type=jnp.float32
    )
    gate_sig = jax.nn.sigmoid(gate_pre)
    gate_act = gate_pre * gate_sig
    partial = jnp.sum(gate_act * up_pre * back_proj, axis=1).reshape(expert_count * dp_count, CAP)
    act_grad = weights[:, None] * back_proj
    d_gate = (act_grad * up_pre * gate_sig * (1.0 + gate_pre * (1.0 - gate_sig))).astype(jnp.bfloat16)
    d_up = (act_grad * gate_act).astype(jnp.bfloat16)
    grad_gate = dot_first(row_block, d_gate).astype(jnp.bfloat16)
    grad_up = dot_first(row_block, d_up).astype(jnp.bfloat16)
    returned = exchange(partial)
    slot_sums = jnp.sum(returned.reshape(expert_count, dp_count, CAP), axis=1)
    value = jnp.sum(jnp.where(select, slot_sums[None], 0.0), axis=2)
    route_grad = jnp.sum(jnp.where(hit, value[:, None, :], 0.0), axis=2)
    return grad_gate[None], grad_up[None], route_grad


PAIR = 2
UNIT = 3 * CAP
PIECES = 4


def move_kernel(
    z_count, ids_hbm, rw_hbm, tok_hbm, cot_hbm, wg_hbm, wu_hbm, wd_hbm,
    rows_ref, dcat_ref, grad_ref, flag_ref,
    ids_ref, rw_ref, tok_ref, cot_ref, wg_ref, wu_ref, wd_ref, send_ref, got_ref, pbuf, rbuf,
    load_sem, y_send, y_recv, up_sem, down_sem, core_sem, recv_sem, back_sem, home_sem,
):
    y_count = 2
    toks, width = tok_ref.shape
    hidden = wg_ref.shape[1]
    piece = width // PIECES
    both = 2 * UNIT
    message = UNIT + 8
    experts = PAIR * y_count
    group = experts * z_count
    me = lax.axis_index("expert")
    z = lax.axis_index("dp")
    y, c = lax.div(me, PAIR), lax.rem(me, PAIR)
    mine = me * z_count + z

    loads = [
        pltpu.make_async_copy(src, dst, load_sem.at[i])
        for i, (src, dst) in enumerate(
            (
                (ids_hbm, ids_ref), (rw_hbm, rw_ref), (tok_hbm, tok_ref), (cot_hbm, cot_ref),
                (wg_hbm, wg_ref), (wu_hbm, wu_ref), (wd_hbm, wd_ref),
            )
        )
    ]
    for load in loads:
        load.start()

    barrier = pltpu.get_barrier_semaphore()
    for step in range(1, group):
        other = lax.rem(mine + step, group)
        pl.semaphore_signal(
            barrier, inc=1, device_id={"expert": lax.div(other, z_count), "dp": lax.rem(other, z_count)},
            device_id_type=pl.DeviceIdType.MESH,
        )

    loads[0].wait()
    loads[1].wait()
    ids = ids_ref[...]
    rw = rw_ref[...].astype(jnp.float32)
    padded = -(-experts // 16) * 16
    number = lax.broadcasted_iota(jnp.int32, (padded, toks), 0)
    chosen = jnp.zeros((padded, toks), jnp.float32)
    for k in range(ids.shape[0]):
        chosen += jnp.where(ids[k : k + 1, :] == number, 1.0, 0.0)
    earlier = lax.broadcasted_iota(jnp.int32, (toks, toks), 0) < lax.broadcasted_iota(jnp.int32, (toks, toks), 1)
    upper = jnp.where(earlier, 1.0, 0.0).astype(jnp.bfloat16)
    rank = jnp.dot(chosen.astype(jnp.bfloat16), upper, preferred_element_type=jnp.float32)
    total = jnp.sum(chosen, axis=1, keepdims=True)
    slot = lax.broadcasted_iota(jnp.int32, (both, toks), 0).astype(jnp.float32)
    lane = lax.broadcasted_iota(jnp.int32, (both, 128), 1)
    select = jnp.zeros((both, toks), jnp.float32)
    tail = jnp.zeros((both, 128), jnp.float32)
    most = jnp.zeros((1, 1), jnp.float32)
    picks = []
    for e in range(experts):
        here = jnp.where(y == e // PAIR, 1.0, 0.0)
        spot = rank[e : e + 1, :]
        if e % PAIR:
            spot = spot + total[e - 1 : e, :]
            most = jnp.maximum(most, total[e - 1 : e, :] + total[e : e + 1, :])
        spot = here * spot + (1.0 - here) * (both - 1.0 - spot)
        pick = jnp.where((slot == spot) & (chosen[e : e + 1, :] > 0.5), 1.0, 0.0)
        weight = jnp.sum(jnp.where(ids == e, rw, 0.0), axis=0, keepdims=True)
        tail += jnp.where(lane == e % PAIR, jnp.sum(pick * weight, axis=1, keepdims=True), 0.0)
        select += pick
        picks.append(pick[:UNIT] + pick[UNIT:])
    select = select.astype(jnp.bfloat16)
    over = jnp.broadcast_to(jnp.where(most > UNIT // 2 + 0.5, 1.0, 0.0), (8, 128))

    def unit(z_src, c_src):
        return pl.multiple_of((z_src * PAIR + c_src) * both, 16)

    def columns(p):
        return pl.ds(p * piece, piece + (128 if p == PIECES - 1 else 0))

    def remote(src, dst, send, recv, target):
        return pltpu.make_async_remote_copy(
            src_ref=src, dst_ref=dst, send_sem=send, recv_sem=recv, device_id=target,
            device_id_type=pl.DeviceIdType.MESH,
        )

    def relay(z_src, p, send, target, c_src=c):
        there = rows_ref.at[pl.ds(unit(z_src, c_src), both), columns(p)]
        return remote(there, there, send, recv_sem.at[z_src, c_src, p], target)

    def to_up(z_src, p):
        return relay(z_src, p, up_sem.at[z_src, p], {"dp": z + 1})

    def to_down(z_src, p):
        return relay(z_src, p, down_sem.at[z_src, p], {"dp": z - 1})

    def to_core(z_src, p):
        return relay(z_src, p, core_sem.at[z_src, p], {"expert": y * PAIR + 1 - c})

    def arrived(z_src, c_src, p):
        relay(z_src, p, load_sem.at[0], {"expert": y * PAIR + 1 - c}, c_src).wait_recv()

    def across(p):
        return remote(
            send_ref.at[:, columns(p)], got_ref.at[:, columns(p)], y_send.at[p], y_recv.at[p],
            {"expert": (1 - y) * PAIR + c},
        )

    own = pl.ds(unit(z, c), both)
    loads[2].wait()
    loads[3].wait()
    for p in range(PIECES):
        at = pl.ds(p * piece, piece)
        x = jnp.dot(select, tok_ref[:, at], preferred_element_type=jnp.float32)
        t = jnp.dot(select, cot_ref[:, at], preferred_element_type=jnp.float32)
        rows_ref[own, at] = jnp.concatenate([x[:UNIT], t[:UNIT]], axis=0).astype(jnp.bfloat16)
        send_ref[:, at] = jnp.concatenate([x[UNIT:], t[UNIT:]], axis=0).astype(jnp.bfloat16)
        if p == PIECES - 1:
            blank = jnp.zeros((UNIT, 128), jnp.float32)
            rows_ref[own, width:] = jnp.concatenate([tail[:UNIT], blank], axis=0).astype(jnp.bfloat16)
            send_ref[:, width:] = jnp.concatenate([tail[UNIT:], blank], axis=0).astype(jnp.bfloat16)
        if p == 0:
            pl.semaphore_wait(barrier, group - 1)
        across(p).start()
    for p in range(PIECES):
        across(p).wait_recv()
        rows_ref[own, columns(p)] = rows_ref[own, columns(p)] + got_ref[:, columns(p)]

        @pl.when(z + 1 < z_count)
        def _(p=p):
            to_up(z, p).start()

        @pl.when(z > 0)
        def _(p=p):
            to_down(z, p).start()

        to_core(z, p).start()

    plane = PAIR * both

    def forward(z_src):
        for p in range(PIECES):
            arrived(z_src, 1 - c, p)
        first = pl.multiple_of(z_src * plane, 16)
        rows = pl.ds(first, plane)

        def add(i, sums):
            at = pl.ds(pl.multiple_of(i * piece, 128), piece)
            x = rows_ref[rows, at]
            return (
                sums[0] + jnp.dot(x, wg_ref[at, :], preferred_element_type=jnp.float32),
                sums[1] + jnp.dot(x, wu_ref[at, :], preferred_element_type=jnp.float32),
                sums[2]
                + lax.dot_general(x, wd_ref[:, at], (((1,), (1,)), ((), ())), preferred_element_type=jnp.float32),
            )

        zero = jnp.zeros((plane, hidden), jnp.float32)
        gates, ups, backs = lax.fori_loop(0, PIECES, add, (zero, zero, zero))
        marks = rows_ref[rows, width:].astype(jnp.float32)
        which = lax.broadcasted_iota(jnp.int32, (UNIT, 128), 1)
        blank = jnp.zeros((UNIT, hidden), jnp.float32)
        for k in range(PAIR):
            low, high = k * both, k * both + UNIT
            gate_pre, up_pre, back = gates[low:high], ups[low:high], backs[high : high + UNIT]
            sig = jax.nn.sigmoid(gate_pre)
            act = gate_pre * sig
            part = jnp.sum(act * up_pre * back, axis=1, keepdims=True)
            start = pl.multiple_of((z_src * PAIR + k) * message, 8)
            pbuf[pl.ds(start, UNIT), :] = jnp.broadcast_to(part, (UNIT, 128))
            pbuf[pl.ds(start + UNIT, 8), :] = over
            weight = jnp.sum(jnp.where(which == c, marks[low:high], 0.0), axis=1, keepdims=True)
            act_grad = weight * back
            d_gate = act_grad * up_pre * sig * (1.0 + gate_pre * (1.0 - sig))
            d_up = act_grad * act
            out = pl.ds(pl.multiple_of(first + k * both, 16), both)
            dcat_ref[out, :hidden] = jnp.concatenate([d_gate, blank], axis=0).astype(jnp.bfloat16)
            dcat_ref[out, hidden:] = jnp.concatenate([d_up, blank], axis=0).astype(jnp.bfloat16)

    def sums_of(z_to, c_to):
        return pbuf.at[pl.ds(pl.multiple_of((z_to * PAIR + c_to) * message, 8), message), :]

    def sums_from(index):
        return rbuf.at[pl.ds(pl.multiple_of(index * message, 8), message), :]

    def home(z_to, c_to, y_to):
        return remote(
            sums_of(z_to, c_to), sums_from(mine), back_sem.at[z_to, c_to, y_to], home_sem.at[mine],
            {"expert": y_to * PAIR + c_to, "dp": z_to},
        )

    def not_me(z_to, c_to, y_to):
        return (z_to != z) | (c_to != c) | (y_to != y)

    def finish(z_src):
        forward(z_src)
        for c_to in range(PAIR):
            for y_to in range(y_count):

                @pl.when(not_me(z_src, c_to, y_to))
                def _(c_to=c_to, y_to=y_to):
                    home(z_src, c_to, y_to).start()

    def finish_hop(hop):
        if hop == 0:
            finish(z)
            return

        @pl.when(z >= hop)
        def _():
            finish(z - hop)

        @pl.when(z + hop < z_count)
        def _():
            finish(z + hop)

    for load in loads[4:]:
        load.wait()
    for hop in range(1, z_count):
        for p in range(PIECES):

            @pl.when(z >= hop)
            def _(p=p, hop=hop):
                arrived(z - hop, c, p)

                @pl.when(z + 1 < z_count)
                def _():
                    to_up(z - hop, p).start()

                to_core(z - hop, p).start()

            @pl.when(z + hop < z_count)
            def _(p=p, hop=hop):
                arrived(z + hop, c, p)

                @pl.when(z > 0)
                def _():
                    to_down(z + hop, p).start()

                to_core(z + hop, p).start()

            if p == 1:
                finish_hop(hop - 1)
    finish_hop(z_count - 1)

    rbuf[pl.ds(pl.multiple_of(mine * message, 8), message), :] = pbuf[
        pl.ds(pl.multiple_of((z * PAIR + c) * message, 8), message), :
    ]

    for p in range(PIECES):
        across(p).wait_send()
        for z_src in range(z_count):
            to_core(z_src, p).wait_send()

            @pl.when((z_src <= z) & (z + 1 < z_count))
            def _(p=p, z_src=z_src):
                to_up(z_src, p).wait_send()

            @pl.when((z_src >= z) & (z > 0))
            def _(p=p, z_src=z_src):
                to_down(z_src, p).wait_send()

    for z_to in range(z_count):
        for c_to in range(PAIR):
            for y_to in range(y_count):

                @pl.when(not_me(z_to, c_to, y_to))
                def _(z_to=z_to, c_to=c_to, y_to=y_to):
                    home(z_to, c_to, y_to).wait_send()
                    index = (y_to * PAIR + c_to) * z_count + z_to
                    remote(
                        sums_from(index), sums_from(index), load_sem.at[0], home_sem.at[index],
                        {"expert": y * PAIR + 1 - c},
                    ).wait_recv()

    result = jnp.zeros(ids.shape, jnp.float32)
    flags = over
    for e in range(experts):
        sums = jnp.zeros((UNIT, 128), jnp.float32)
        for k in range(z_count):
            first = (e * z_count + k) * message
            sums = sums + rbuf[first : first + UNIT, :]
            flags = jnp.maximum(flags, rbuf[first + UNIT : first + message, :])
        value = jnp.sum(picks[e] * sums, axis=0, keepdims=True)
        result += jnp.where(ids == e, value, 0.0)
    grad_ref[...] = result
    flag_ref[...] = flags


def back_kernel(rows_ref, dcat_ref, gate_ref, up_ref):
    hidden = gate_ref.shape[1]
    both = dot_first(rows_ref[...], dcat_ref[...]).astype(jnp.bfloat16)
    gate_ref[...] = both[:, :hidden]
    up_ref[...] = both[:, hidden:]


def moved(*args):
    tokens, cotangent, route_ids, route_weight, gate_weight, up_weight, down_weight = args
    y_count = lax.axis_size("expert") // PAIR
    z_count = lax.axis_size("dp")
    tok_count, width = tokens.shape
    hidden = gate_weight.shape[2]
    both = 2 * UNIT
    units = PAIR * z_count
    group = units * y_count
    message = UNIT + 8
    dma = pltpu.SemaphoreType.DMA
    rows, dcat, grad, flag = pl.pallas_call(
        functools.partial(move_kernel, z_count),
        out_shape=(
            jax.ShapeDtypeStruct((units * both, width + 128), jnp.bfloat16),
            jax.ShapeDtypeStruct((units * both, 2 * hidden), jnp.bfloat16),
            jax.ShapeDtypeStruct(route_ids.shape[::-1], jnp.float32),
            jax.ShapeDtypeStruct((8, 128), jnp.float32),
        ),
        in_specs=[pl.BlockSpec(memory_space=pl.ANY)] * 7,
        out_specs=[pl.BlockSpec(memory_space=pltpu.VMEM)] * 4,
        scratch_shapes=[
            pltpu.VMEM(route_ids.shape[::-1], jnp.int32),
            pltpu.VMEM(route_ids.shape[::-1], jnp.float32),
            pltpu.VMEM((tok_count, width), jnp.bfloat16),
            pltpu.VMEM((tok_count, width), jnp.bfloat16),
            pltpu.VMEM((width, hidden), jnp.bfloat16),
            pltpu.VMEM((width, hidden), jnp.bfloat16),
            pltpu.VMEM((hidden, width), jnp.bfloat16),
            pltpu.VMEM((both, width + 128), jnp.bfloat16),
            pltpu.VMEM((both, width + 128), jnp.bfloat16),
            pltpu.VMEM((units * message, 128), jnp.float32),
            pltpu.VMEM((group * message, 128), jnp.float32),
            dma((7,)),
            dma((PIECES,)),
            dma((PIECES,)),
            dma((z_count, PIECES)),
            dma((z_count, PIECES)),
            dma((z_count, PIECES)),
            dma((z_count, PAIR, PIECES)),
            dma((z_count, PAIR, y_count)),
            dma((group,)),
        ],
        compiler_params=pltpu.CompilerParams(
            collective_id=0, has_side_effects=True, vmem_limit_bytes=60 * 2**20
        ),
        cost_estimate=pl.CostEstimate(
            flops=6 * units * both * width * hidden,
            bytes_accessed=8 * width * hidden,
            transcendentals=units * UNIT * hidden,
        ),
    )(
        route_ids.T, route_weight.T.astype(jnp.float32), tokens, cotangent,
        gate_weight[0], up_weight[0], down_weight[0],
    )

    def fitting():
        tile = math.gcd(width, 1024)
        gate, up = pl.pallas_call(
            back_kernel,
            out_shape=(jax.ShapeDtypeStruct((width, hidden), jnp.bfloat16),) * 2,
            grid=(width // tile,),
            in_specs=[
                pl.BlockSpec((units * both, tile), lambda i: (0, i)),
                pl.BlockSpec((units * both, 2 * hidden), lambda i: (0, 0)),
            ],
            out_specs=(pl.BlockSpec((tile, hidden), lambda i: (i, 0)),) * 2,
            compiler_params=pltpu.CompilerParams(vmem_limit_bytes=60 * 2**20),
        )(rows, dcat)
        return gate[None], up[None], grad.T

    return lax.cond(flag[0, 0] > 0.5, lambda: general(*args), fitting)


def fits(mesh):
    return mesh.shape["expert"] == 2 * PAIR and mesh.shape["dp"] <= 8


def solution(mesh):
    return jax.shard_map(
        moved if fits(mesh) else general,
        mesh=mesh,
        in_specs=(
            P(("groups", "expert", "dp"), None),
            P(("groups", "expert", "dp"), None),
            P(("groups", "expert", "dp"), None),
            P(("groups", "expert", "dp"), None),
            P("expert", None, "dp"),
            P("expert", None, "dp"),
            P("expert", "dp", None),
        ),
        out_specs=(
            P(("groups", "expert"), None, "dp"),
            P(("groups", "expert"), None, "dp"),
            P(("groups", "expert", "dp"), None),
        ),
        check_vma=False,
    )
```

```python
import functools
import math

import jax
import jax.numpy as jnp
from jax import lax
from jax.experimental import pallas as pl
from jax.experimental.pallas import tpu as pltpu
from jax.sharding import PartitionSpec as P

CAP = 8


def dot_first(a, b):
    return lax.dot_general(a, b, (((0,), (0,)), ((), ())), preferred_element_type=jnp.float32)


def general(tokens, cotangent, route_ids, route_weight, gate_weight, up_weight, down_weight):
    expert_count = lax.axis_size("expert")
    dp_count = lax.axis_size("dp")
    tok_count, model_width = tokens.shape
    experts = jnp.arange(expert_count, dtype=jnp.int32)
    hit = route_ids[:, :, None] == experts[None, None, :]
    chosen = jnp.any(hit, axis=1)
    weight_tok = jnp.sum(jnp.where(hit, route_weight.astype(jnp.float32)[:, :, None], 0.0), axis=1)
    row = jnp.arange(tok_count, dtype=jnp.int32)
    earlier = (row[None, :] < row[:, None]).astype(jnp.bfloat16)
    rank = jnp.dot(earlier, chosen.astype(jnp.bfloat16), preferred_element_type=jnp.float32).astype(jnp.int32)
    place = jnp.arange(CAP, dtype=jnp.int32)
    select = chosen[:, :, None] & (rank[:, :, None] == place[None, None, :])
    onehot = select.reshape(tok_count, expert_count * CAP).astype(jnp.bfloat16)
    send_weight = jnp.sum(jnp.where(select, weight_tok[:, :, None], 0.0), axis=0).astype(jnp.bfloat16)
    send_rows = dot_first(onehot, tokens).astype(jnp.bfloat16).reshape(expert_count, CAP, model_width)
    send_cots = dot_first(onehot, cotangent).astype(jnp.bfloat16).reshape(expert_count, CAP, model_width)

    def widen_rows(array):
        spread = jnp.broadcast_to(array[:, None], (expert_count, dp_count) + array.shape[1:])
        return spread.reshape((expert_count * dp_count,) + array.shape[1:])

    def exchange(array):
        return lax.all_to_all(array, ("expert", "dp"), split_axis=0, concat_axis=0, tiled=True)

    row_block = exchange(widen_rows(send_rows)).reshape(-1, model_width)
    cot_block = exchange(widen_rows(send_cots)).reshape(-1, model_width)
    weights = exchange(widen_rows(send_weight)).reshape(-1).astype(jnp.float32)
    gate_pre = jnp.dot(row_block, gate_weight[0], preferred_element_type=jnp.float32)
    up_pre = jnp.dot(row_block, up_weight[0], preferred_element_type=jnp.float32)
    back_proj = lax.dot_general(
        cot_block, down_weight[0], (((1,), (1,)), ((), ())), preferred_element_type=jnp.float32
    )
    gate_sig = jax.nn.sigmoid(gate_pre)
    gate_act = gate_pre * gate_sig
    partial = jnp.sum(gate_act * up_pre * back_proj, axis=1).reshape(expert_count * dp_count, CAP)
    act_grad = weights[:, None] * back_proj
    d_gate = (act_grad * up_pre * gate_sig * (1.0 + gate_pre * (1.0 - gate_sig))).astype(jnp.bfloat16)
    d_up = (act_grad * gate_act).astype(jnp.bfloat16)
    grad_gate = dot_first(row_block, d_gate).astype(jnp.bfloat16)
    grad_up = dot_first(row_block, d_up).astype(jnp.bfloat16)
    returned = exchange(partial)
    slot_sums = jnp.sum(returned.reshape(expert_count, dp_count, CAP), axis=1)
    value = jnp.sum(jnp.where(select, slot_sums[None], 0.0), axis=2)
    route_grad = jnp.sum(jnp.where(hit, value[:, None, :], 0.0), axis=2)
    return grad_gate[None], grad_up[None], route_grad


PAIR = 2
UNIT = 3 * CAP
PIECES = 4


def move_kernel(
    z_count, ids_hbm, rw_hbm, tok_hbm, cot_hbm, wg_hbm, wu_hbm, wd_hbm,
    kept_ref, dcat_ref, grad_ref, flag_ref,
    rows_ref, ids_ref, rw_ref, tok_ref, cot_ref, wg_ref, wu_ref, wd_ref, send_ref, got_ref, pbuf, rbuf,
    load_sem, y_send, y_recv, up_sem, down_sem, core_sem, recv_sem, back_sem, home_sem,
):
    y_count = 2
    toks, width = tok_ref.shape
    hidden = wg_ref.shape[1]
    piece = width // PIECES
    both = 2 * UNIT
    message = UNIT + 8
    experts = PAIR * y_count
    group = experts * z_count
    me = lax.axis_index("expert")
    z = lax.axis_index("dp")
    y, c = lax.div(me, PAIR), lax.rem(me, PAIR)
    mine = me * z_count + z

    loads = [
        pltpu.make_async_copy(src, dst, load_sem.at[i])
        for i, (src, dst) in enumerate(
            (
                (ids_hbm, ids_ref), (rw_hbm, rw_ref), (tok_hbm, tok_ref), (cot_hbm, cot_ref),
                (wg_hbm, wg_ref), (wu_hbm, wu_ref), (wd_hbm, wd_ref),
            )
        )
    ]
    for load in loads:
        load.start()

    barrier = pltpu.get_barrier_semaphore()
    for step in range(1, group):
        other = lax.rem(mine + step, group)
        pl.semaphore_signal(
            barrier, inc=1, device_id={"expert": lax.div(other, z_count), "dp": lax.rem(other, z_count)},
            device_id_type=pl.DeviceIdType.MESH,
        )

    loads[0].wait()
    loads[1].wait()
    ids = ids_ref[...]
    rw = rw_ref[...].astype(jnp.float32)
    padded = -(-experts // 16) * 16
    number = lax.broadcasted_iota(jnp.int32, (padded, toks), 0)
    chosen = jnp.zeros((padded, toks), jnp.float32)
    for k in range(ids.shape[0]):
        chosen += jnp.where(ids[k : k + 1, :] == number, 1.0, 0.0)
    earlier = lax.broadcasted_iota(jnp.int32, (toks, toks), 0) < lax.broadcasted_iota(jnp.int32, (toks, toks), 1)
    upper = jnp.where(earlier, 1.0, 0.0).astype(jnp.bfloat16)
    rank = jnp.dot(chosen.astype(jnp.bfloat16), upper, preferred_element_type=jnp.float32)
    total = jnp.sum(chosen, axis=1, keepdims=True)
    slot = lax.broadcasted_iota(jnp.int32, (both, toks), 0).astype(jnp.float32)
    lane = lax.broadcasted_iota(jnp.int32, (both, 128), 1)
    select = jnp.zeros((both, toks), jnp.float32)
    tail = jnp.zeros((both, 128), jnp.float32)
    most = jnp.zeros((1, 1), jnp.float32)
    picks = []
    for e in range(experts):
        here = jnp.where(y == e // PAIR, 1.0, 0.0)
        spot = rank[e : e + 1, :]
        if e % PAIR:
            spot = spot + total[e - 1 : e, :]
            most = jnp.maximum(most, total[e - 1 : e, :] + total[e : e + 1, :])
        spot = here * spot + (1.0 - here) * (both - 1.0 - spot)
        pick = jnp.where((slot == spot) & (chosen[e : e + 1, :] > 0.5), 1.0, 0.0)
        weight = jnp.sum(jnp.where(ids == e, rw, 0.0), axis=0, keepdims=True)
        tail += jnp.where(lane == e % PAIR, jnp.sum(pick * weight, axis=1, keepdims=True), 0.0)
        select += pick
        picks.append(pick[:UNIT] + pick[UNIT:])
    select = select.astype(jnp.bfloat16)
    over = jnp.broadcast_to(jnp.where(most > UNIT // 2 + 0.5, 1.0, 0.0), (8, 128))

    def unit(z_src, c_src):
        return pl.multiple_of((z_src * PAIR + c_src) * both, 16)

    def columns(p):
        return pl.ds(p * piece, piece + (128 if p == PIECES - 1 else 0))

    def remote(src, dst, send, recv, target):
        return pltpu.make_async_remote_copy(
            src_ref=src, dst_ref=dst, send_sem=send, recv_sem=recv, device_id=target,
            device_id_type=pl.DeviceIdType.MESH,
        )

    def relay(z_src, p, send, target, c_src=c):
        there = rows_ref.at[pl.ds(unit(z_src, c_src), both), columns(p)]
        return remote(there, there, send, recv_sem.at[z_src, c_src, p], target)

    def to_up(z_src, p):
        return relay(z_src, p, up_sem.at[z_src, p], {"dp": z + 1})

    def to_down(z_src, p):
        return relay(z_src, p, down_sem.at[z_src, p], {"dp": z - 1})

    def to_core(z_src, p):
        return relay(z_src, p, core_sem.at[z_src, p], {"expert": y * PAIR + 1 - c})

    def arrived(z_src, c_src, p):
        relay(z_src, p, load_sem.at[0], {"expert": y * PAIR + 1 - c}, c_src).wait_recv()

    def across(p):
        return remote(
            send_ref.at[:, columns(p)], got_ref.at[:, columns(p)], y_send.at[p], y_recv.at[p],
            {"expert": (1 - y) * PAIR + c},
        )

    own = pl.ds(unit(z, c), both)
    loads[2].wait()
    loads[3].wait()
    for p in range(PIECES):
        at = pl.ds(p * piece, piece)
        x = jnp.dot(select, tok_ref[:, at], preferred_element_type=jnp.float32)
        t = jnp.dot(select, cot_ref[:, at], preferred_element_type=jnp.float32)
        rows_ref[own, at] = jnp.concatenate([x[:UNIT], t[:UNIT]], axis=0).astype(jnp.bfloat16)
        send_ref[:, at] = jnp.concatenate([x[UNIT:], t[UNIT:]], axis=0).astype(jnp.bfloat16)
        if p == PIECES - 1:
            blank = jnp.zeros((UNIT, 128), jnp.float32)
            rows_ref[own, width:] = jnp.concatenate([tail[:UNIT], blank], axis=0).astype(jnp.bfloat16)
            send_ref[:, width:] = jnp.concatenate([tail[UNIT:], blank], axis=0).astype(jnp.bfloat16)
        if p == 0:
            pl.semaphore_wait(barrier, group - 1)
        across(p).start()
    for p in range(PIECES):
        across(p).wait_recv()
        rows_ref[own, columns(p)] = rows_ref[own, columns(p)] + got_ref[:, columns(p)]

        @pl.when(z + 1 < z_count)
        def _(p=p):
            to_up(z, p).start()

        @pl.when(z > 0)
        def _(p=p):
            to_down(z, p).start()

        to_core(z, p).start()

    plane = PAIR * both

    def forward(z_src):
        for p in range(PIECES):
            arrived(z_src, 1 - c, p)
        first = pl.multiple_of(z_src * plane, 16)
        rows = pl.ds(first, plane)

        def add(i, sums):
            at = pl.ds(pl.multiple_of(i * piece, 128), piece)
            x = rows_ref[rows, at]
            kept_ref[pl.ds(pl.multiple_of(z_src * both, 16), both), at] = jnp.concatenate(
                [x[:UNIT], x[both : both + UNIT]], axis=0
            )
            return (
                sums[0] + jnp.dot(x, wg_ref[at, :], preferred_element_type=jnp.float32),
                sums[1] + jnp.dot(x, wu_ref[at, :], preferred_element_type=jnp.float32),
                sums[2]
                + lax.dot_general(x, wd_ref[:, at], (((1,), (1,)), ((), ())), preferred_element_type=jnp.float32),
            )

        zero = jnp.zeros((plane, hidden), jnp.float32)
        gates, ups, backs = lax.fori_loop(0, PIECES, add, (zero, zero, zero))
        marks = rows_ref[rows, width:].astype(jnp.float32)
        which = lax.broadcasted_iota(jnp.int32, (UNIT, 128), 1)
        gate_parts, up_parts = [], []
        for k in range(PAIR):
            low, high = k * both, k * both + UNIT
            gate_pre, up_pre, back = gates[low:high], ups[low:high], backs[high : high + UNIT]
            sig = jax.nn.sigmoid(gate_pre)
            act = gate_pre * sig
            part = jnp.sum(act * up_pre * back, axis=1, keepdims=True)
            start = pl.multiple_of((z_src * PAIR + k) * message, 8)
            pbuf[pl.ds(start, UNIT), :] = jnp.broadcast_to(part, (UNIT, 128))
            pbuf[pl.ds(start + UNIT, 8), :] = over
            weight = jnp.sum(jnp.where(which == c, marks[low:high], 0.0), axis=1, keepdims=True)
            act_grad = weight * back
            d_gate = act_grad * up_pre * sig * (1.0 + gate_pre * (1.0 - sig))
            d_up = act_grad * act
            gate_parts.append(d_gate)
            up_parts.append(d_up)
        out = pl.ds(pl.multiple_of(z_src * both, 16), both)
        dcat_ref[out, :hidden] = jnp.concatenate(gate_parts, axis=0).astype(jnp.bfloat16)
        dcat_ref[out, hidden:] = jnp.concatenate(up_parts, axis=0).astype(jnp.bfloat16)

    def sums_of(z_to, c_to):
        return pbuf.at[pl.ds(pl.multiple_of((z_to * PAIR + c_to) * message, 8), message), :]

    def sums_from(index):
        return rbuf.at[pl.ds(pl.multiple_of(index * message, 8), message), :]

    def home(z_to, c_to, y_to):
        return remote(
            sums_of(z_to, c_to), sums_from(mine), back_sem.at[z_to, c_to, y_to], home_sem.at[mine],
            {"expert": y_to * PAIR + c_to, "dp": z_to},
        )

    def not_me(z_to, c_to, y_to):
        return (z_to != z) | (c_to != c) | (y_to != y)

    def finish(z_src):
        forward(z_src)
        for c_to in range(PAIR):
            for y_to in range(y_count):

                @pl.when(not_me(z_src, c_to, y_to))
                def _(c_to=c_to, y_to=y_to):
                    home(z_src, c_to, y_to).start()

    def finish_hop(hop):
        if hop == 0:
            finish(z)
            return

        @pl.when(z >= hop)
        def _():
            finish(z - hop)

        @pl.when(z + hop < z_count)
        def _():
            finish(z + hop)

    for load in loads[4:]:
        load.wait()
    for hop in range(1, z_count):
        for p in range(PIECES):

            @pl.when(z >= hop)
            def _(p=p, hop=hop):
                arrived(z - hop, c, p)

                @pl.when(z + 1 < z_count)
                def _():
                    to_up(z - hop, p).start()

                to_core(z - hop, p).start()

            @pl.when(z + hop < z_count)
            def _(p=p, hop=hop):
                arrived(z + hop, c, p)

                @pl.when(z > 0)
                def _():
                    to_down(z + hop, p).start()

                to_core(z + hop, p).start()

            if p == 1:
                finish_hop(hop - 1)
    finish_hop(z_count - 1)

    rbuf[pl.ds(pl.multiple_of(mine * message, 8), message), :] = pbuf[
        pl.ds(pl.multiple_of((z * PAIR + c) * message, 8), message), :
    ]

    for p in range(PIECES):
        across(p).wait_send()
        for z_src in range(z_count):
            to_core(z_src, p).wait_send()

            @pl.when((z_src <= z) & (z + 1 < z_count))
            def _(p=p, z_src=z_src):
                to_up(z_src, p).wait_send()

            @pl.when((z_src >= z) & (z > 0))
            def _(p=p, z_src=z_src):
                to_down(z_src, p).wait_send()

    for z_to in range(z_count):
        for c_to in range(PAIR):
            for y_to in range(y_count):

                @pl.when(not_me(z_to, c_to, y_to))
                def _(z_to=z_to, c_to=c_to, y_to=y_to):
                    home(z_to, c_to, y_to).wait_send()
                    index = (y_to * PAIR + c_to) * z_count + z_to
                    remote(
                        sums_from(index), sums_from(index), load_sem.at[0], home_sem.at[index],
                        {"expert": y * PAIR + 1 - c},
                    ).wait_recv()

    result = jnp.zeros(ids.shape, jnp.float32)
    flags = over
    for e in range(experts):
        sums = jnp.zeros((UNIT, 128), jnp.float32)
        for k in range(z_count):
            first = (e * z_count + k) * message
            sums = sums + rbuf[first : first + UNIT, :]
            flags = jnp.maximum(flags, rbuf[first + UNIT : first + message, :])
        value = jnp.sum(picks[e] * sums, axis=0, keepdims=True)
        result += jnp.where(ids == e, value, 0.0)
    grad_ref[...] = result
    flag_ref[...] = flags


def back_kernel(rows_ref, dcat_ref, gate_ref, up_ref):
    hidden = gate_ref.shape[1]
    both = dot_first(rows_ref[...], dcat_ref[...]).astype(jnp.bfloat16)
    gate_ref[...] = both[:, :hidden]
    up_ref[...] = both[:, hidden:]


def moved(*args):
    tokens, cotangent, route_ids, route_weight, gate_weight, up_weight, down_weight = args
    y_count = lax.axis_size("expert") // PAIR
    z_count = lax.axis_size("dp")
    tok_count, width = tokens.shape
    hidden = gate_weight.shape[2]
    both = 2 * UNIT
    units = PAIR * z_count
    group = units * y_count
    message = UNIT + 8
    dma = pltpu.SemaphoreType.DMA
    rows, dcat, grad, flag = pl.pallas_call(
        functools.partial(move_kernel, z_count),
        out_shape=(
            jax.ShapeDtypeStruct((units * UNIT, width), jnp.bfloat16),
            jax.ShapeDtypeStruct((units * UNIT, 2 * hidden), jnp.bfloat16),
            jax.ShapeDtypeStruct(route_ids.shape[::-1], jnp.float32),
            jax.ShapeDtypeStruct((8, 128), jnp.float32),
        ),
        in_specs=[pl.BlockSpec(memory_space=pl.ANY)] * 7,
        out_specs=[pl.BlockSpec(memory_space=pltpu.VMEM)] * 4,
        scratch_shapes=[
            pltpu.VMEM((units * both, width + 128), jnp.bfloat16),
            pltpu.VMEM(route_ids.shape[::-1], jnp.int32),
            pltpu.VMEM(route_ids.shape[::-1], jnp.float32),
            pltpu.VMEM((tok_count, width), jnp.bfloat16),
            pltpu.VMEM((tok_count, width), jnp.bfloat16),
            pltpu.VMEM((width, hidden), jnp.bfloat16),
            pltpu.VMEM((width, hidden), jnp.bfloat16),
            pltpu.VMEM((hidden, width), jnp.bfloat16),
            pltpu.VMEM((both, width + 128), jnp.bfloat16),
            pltpu.VMEM((both, width + 128), jnp.bfloat16),
            pltpu.VMEM((units * message, 128), jnp.float32),
            pltpu.VMEM((group * message, 128), jnp.float32),
            dma((7,)),
            dma((PIECES,)),
            dma((PIECES,)),
            dma((z_count, PIECES)),
            dma((z_count, PIECES)),
            dma((z_count, PIECES)),
            dma((z_count, PAIR, PIECES)),
            dma((z_count, PAIR, y_count)),
            dma((group,)),
        ],
        compiler_params=pltpu.CompilerParams(
            collective_id=0, has_side_effects=True, vmem_limit_bytes=60 * 2**20
        ),
        cost_estimate=pl.CostEstimate(
            flops=6 * units * both * width * hidden,
            bytes_accessed=8 * width * hidden,
            transcendentals=units * UNIT * hidden,
        ),
    )(
        route_ids.T, route_weight.T.astype(jnp.float32), tokens, cotangent,
        gate_weight[0], up_weight[0], down_weight[0],
    )

    def fitting():
        tile = math.gcd(width, 1024)
        gate, up = pl.pallas_call(
            back_kernel,
            out_shape=(jax.ShapeDtypeStruct((width, hidden), jnp.bfloat16),) * 2,
            grid=(width // tile,),
            in_specs=[
                pl.BlockSpec((units * UNIT, tile), lambda i: (0, i)),
                pl.BlockSpec((units * UNIT, 2 * hidden), lambda i: (0, 0)),
            ],
            out_specs=(pl.BlockSpec((tile, hidden), lambda i: (i, 0)),) * 2,
            compiler_params=pltpu.CompilerParams(vmem_limit_bytes=60 * 2**20),
        )(rows, dcat)
        return gate[None], up[None], grad.T

    return lax.cond(flag[0, 0] > 0.5, lambda: general(*args), fitting)


def fits(mesh):
    return mesh.shape["expert"] == 2 * PAIR and mesh.shape["dp"] <= 8


def solution(mesh):
    return jax.shard_map(
        moved if fits(mesh) else general,
        mesh=mesh,
        in_specs=(
            P(("groups", "expert", "dp"), None),
            P(("groups", "expert", "dp"), None),
            P(("groups", "expert", "dp"), None),
            P(("groups", "expert", "dp"), None),
            P("expert", None, "dp"),
            P("expert", None, "dp"),
            P("expert", "dp", None),
        ),
        out_specs=(
            P(("groups", "expert"), None, "dp"),
            P(("groups", "expert"), None, "dp"),
            P(("groups", "expert", "dp"), None),
        ),
        check_vma=False,
    )
```

```python
import functools
import math

import jax
import jax.numpy as jnp
from jax import lax
from jax.experimental import pallas as pl
from jax.experimental.pallas import tpu as pltpu
from jax.sharding import PartitionSpec as P

CAP = 8


def dot_first(a, b):
    return lax.dot_general(a, b, (((0,), (0,)), ((), ())), preferred_element_type=jnp.float32)


def general(tokens, cotangent, route_ids, route_weight, gate_weight, up_weight, down_weight):
    expert_count = lax.axis_size("expert")
    dp_count = lax.axis_size("dp")
    tok_count, model_width = tokens.shape
    experts = jnp.arange(expert_count, dtype=jnp.int32)
    hit = route_ids[:, :, None] == experts[None, None, :]
    chosen = jnp.any(hit, axis=1)
    weight_tok = jnp.sum(jnp.where(hit, route_weight.astype(jnp.float32)[:, :, None], 0.0), axis=1)
    row = jnp.arange(tok_count, dtype=jnp.int32)
    earlier = (row[None, :] < row[:, None]).astype(jnp.bfloat16)
    rank = jnp.dot(earlier, chosen.astype(jnp.bfloat16), preferred_element_type=jnp.float32).astype(jnp.int32)
    place = jnp.arange(CAP, dtype=jnp.int32)
    select = chosen[:, :, None] & (rank[:, :, None] == place[None, None, :])
    onehot = select.reshape(tok_count, expert_count * CAP).astype(jnp.bfloat16)
    send_weight = jnp.sum(jnp.where(select, weight_tok[:, :, None], 0.0), axis=0).astype(jnp.bfloat16)
    send_rows = dot_first(onehot, tokens).astype(jnp.bfloat16).reshape(expert_count, CAP, model_width)
    send_cots = dot_first(onehot, cotangent).astype(jnp.bfloat16).reshape(expert_count, CAP, model_width)

    def widen_rows(array):
        spread = jnp.broadcast_to(array[:, None], (expert_count, dp_count) + array.shape[1:])
        return spread.reshape((expert_count * dp_count,) + array.shape[1:])

    def exchange(array):
        return lax.all_to_all(array, ("expert", "dp"), split_axis=0, concat_axis=0, tiled=True)

    row_block = exchange(widen_rows(send_rows)).reshape(-1, model_width)
    cot_block = exchange(widen_rows(send_cots)).reshape(-1, model_width)
    weights = exchange(widen_rows(send_weight)).reshape(-1).astype(jnp.float32)
    gate_pre = jnp.dot(row_block, gate_weight[0], preferred_element_type=jnp.float32)
    up_pre = jnp.dot(row_block, up_weight[0], preferred_element_type=jnp.float32)
    back_proj = lax.dot_general(
        cot_block, down_weight[0], (((1,), (1,)), ((), ())), preferred_element_type=jnp.float32
    )
    gate_sig = jax.nn.sigmoid(gate_pre)
    gate_act = gate_pre * gate_sig
    partial = jnp.sum(gate_act * up_pre * back_proj, axis=1).reshape(expert_count * dp_count, CAP)
    act_grad = weights[:, None] * back_proj
    d_gate = (act_grad * up_pre * gate_sig * (1.0 + gate_pre * (1.0 - gate_sig))).astype(jnp.bfloat16)
    d_up = (act_grad * gate_act).astype(jnp.bfloat16)
    grad_gate = dot_first(row_block, d_gate).astype(jnp.bfloat16)
    grad_up = dot_first(row_block, d_up).astype(jnp.bfloat16)
    returned = exchange(partial)
    slot_sums = jnp.sum(returned.reshape(expert_count, dp_count, CAP), axis=1)
    value = jnp.sum(jnp.where(select, slot_sums[None], 0.0), axis=2)
    route_grad = jnp.sum(jnp.where(hit, value[:, None, :], 0.0), axis=2)
    return grad_gate[None], grad_up[None], route_grad


PAIR = 2
UNIT = 3 * CAP
PIECES = 4


def move_kernel(
    z_count, ids_hbm, rw_ref, tok_hbm, cot_hbm, wg_hbm, wu_hbm, wd_hbm,
    kept_ref, dcat_ref, grad_ref, flag_ref,
    rows_ref, ids_ref, tok_ref, cot_ref, wg_ref, wu_ref, wd_ref, send_ref, got_ref, pbuf, rbuf,
    load_sem, y_send, y_recv, up_sem, down_sem, core_sem, recv_sem, back_sem, home_sem,
):
    y_count = 2
    toks, width = tok_ref.shape
    hidden = wg_ref.shape[1]
    piece = width // PIECES
    both = 2 * UNIT
    message = UNIT + 8
    experts = PAIR * y_count
    group = experts * z_count
    me = lax.axis_index("expert")
    z = lax.axis_index("dp")
    y, c = lax.div(me, PAIR), lax.rem(me, PAIR)
    mine = me * z_count + z

    loads = [
        pltpu.make_async_copy(src, dst, load_sem.at[i])
        for i, (src, dst) in enumerate(
            (
                (ids_hbm, ids_ref), (tok_hbm, tok_ref), (cot_hbm, cot_ref),
                (wg_hbm, wg_ref), (wu_hbm, wu_ref), (wd_hbm, wd_ref),
            )
        )
    ]
    for load in loads[:3]:
        load.start()

    barrier = pltpu.get_barrier_semaphore()
    for step in range(1, group):
        other = lax.rem(mine + step, group)
        pl.semaphore_signal(
            barrier, inc=1, device_id={"expert": lax.div(other, z_count), "dp": lax.rem(other, z_count)},
            device_id_type=pl.DeviceIdType.MESH,
        )

    loads[0].wait()
    ids = ids_ref[...]
    rw = rw_ref[...].astype(jnp.float32)
    padded = -(-experts // 16) * 16
    number = lax.broadcasted_iota(jnp.int32, (padded, toks), 0)
    chosen = jnp.zeros((padded, toks), jnp.float32)
    for k in range(ids.shape[0]):
        chosen += jnp.where(ids[k : k + 1, :] == number, 1.0, 0.0)
    earlier = lax.broadcasted_iota(jnp.int32, (toks, toks), 0) < lax.broadcasted_iota(jnp.int32, (toks, toks), 1)
    upper = jnp.where(earlier, 1.0, 0.0).astype(jnp.bfloat16)
    rank = jnp.dot(chosen.astype(jnp.bfloat16), upper, preferred_element_type=jnp.float32)
    total = jnp.sum(chosen, axis=1, keepdims=True)
    slot = lax.broadcasted_iota(jnp.int32, (both, toks), 0).astype(jnp.float32)
    lane = lax.broadcasted_iota(jnp.int32, (both, 128), 1)
    select = jnp.zeros((both, toks), jnp.float32)
    tail = jnp.zeros((both, 128), jnp.float32)
    most = jnp.zeros((1, 1), jnp.float32)
    picks = []
    for e in range(experts):
        here = jnp.where(y == e // PAIR, 1.0, 0.0)
        spot = rank[e : e + 1, :]
        if e % PAIR:
            spot = spot + total[e - 1 : e, :]
            most = jnp.maximum(most, total[e - 1 : e, :] + total[e : e + 1, :])
        spot = here * spot + (1.0 - here) * (both - 1.0 - spot)
        pick = jnp.where((slot == spot) & (chosen[e : e + 1, :] > 0.5), 1.0, 0.0)
        weight = jnp.sum(jnp.where(ids == e, rw, 0.0), axis=0, keepdims=True)
        tail += jnp.where(lane == e % PAIR, jnp.sum(pick * weight, axis=1, keepdims=True), 0.0)
        select += pick
        picks.append(pick[:UNIT] + pick[UNIT:])
    select = select.astype(jnp.bfloat16)
    over = jnp.broadcast_to(jnp.where(most > UNIT // 2 + 0.5, 1.0, 0.0), (8, 128))

    def unit(z_src, c_src):
        return pl.multiple_of((z_src * PAIR + c_src) * both, 16)

    def columns(p):
        return pl.ds(p * piece, piece + (128 if p == PIECES - 1 else 0))

    def remote(src, dst, send, recv, target):
        return pltpu.make_async_remote_copy(
            src_ref=src, dst_ref=dst, send_sem=send, recv_sem=recv, device_id=target,
            device_id_type=pl.DeviceIdType.MESH,
        )

    def relay(z_src, p, send, target, c_src=c):
        there = rows_ref.at[pl.ds(unit(z_src, c_src), both), columns(p)]
        return remote(there, there, send, recv_sem.at[z_src, c_src, p], target)

    def to_up(z_src, p):
        return relay(z_src, p, up_sem.at[z_src, p], {"dp": z + 1})

    def to_down(z_src, p):
        return relay(z_src, p, down_sem.at[z_src, p], {"dp": z - 1})

    def to_core(z_src, p):
        return relay(z_src, p, core_sem.at[z_src, p], {"expert": y * PAIR + 1 - c})

    def arrived(z_src, c_src, p):
        relay(z_src, p, load_sem.at[0], {"expert": y * PAIR + 1 - c}, c_src).wait_recv()

    def across(p):
        return remote(
            send_ref.at[:, columns(p)], got_ref.at[:, columns(p)], y_send.at[p], y_recv.at[p],
            {"expert": (1 - y) * PAIR + c},
        )

    own = pl.ds(unit(z, c), both)
    loads[1].wait()
    loads[2].wait()
    for load in loads[3:]:
        load.start()
    for p in range(PIECES):
        at = pl.ds(p * piece, piece)
        x = jnp.dot(select, tok_ref[:, at], preferred_element_type=jnp.float32)
        t = jnp.dot(select, cot_ref[:, at], preferred_element_type=jnp.float32)
        rows_ref[own, at] = jnp.concatenate([x[:UNIT], t[:UNIT]], axis=0).astype(jnp.bfloat16)
        send_ref[:, at] = jnp.concatenate([x[UNIT:], t[UNIT:]], axis=0).astype(jnp.bfloat16)
        if p == PIECES - 1:
            blank = jnp.zeros((UNIT, 128), jnp.float32)
            rows_ref[own, width:] = jnp.concatenate([tail[:UNIT], blank], axis=0).astype(jnp.bfloat16)
            send_ref[:, width:] = jnp.concatenate([tail[UNIT:], blank], axis=0).astype(jnp.bfloat16)
        if p == 0:
            pl.semaphore_wait(barrier, group - 1)
        across(p).start()
    for p in range(PIECES):
        across(p).wait_recv()
        rows_ref[own, columns(p)] = rows_ref[own, columns(p)] + got_ref[:, columns(p)]

        @pl.when(z + 1 < z_count)
        def _(p=p):
            to_up(z, p).start()

        @pl.when(z > 0)
        def _(p=p):
            to_down(z, p).start()

        to_core(z, p).start()

    plane = PAIR * both

    def forward(z_src):
        for p in range(PIECES):
            arrived(z_src, 1 - c, p)
        first = pl.multiple_of(z_src * plane, 16)
        rows = pl.ds(first, plane)

        def add(i, sums):
            at = pl.ds(pl.multiple_of(i * piece, 128), piece)
            x = rows_ref[rows, at]
            kept_ref[pl.ds(pl.multiple_of(z_src * both, 16), both), at] = jnp.concatenate(
                [x[:UNIT], x[both : both + UNIT]], axis=0
            )
            return (
                sums[0] + jnp.dot(x, wg_ref[at, :], preferred_element_type=jnp.float32),
                sums[1] + jnp.dot(x, wu_ref[at, :], preferred_element_type=jnp.float32),
                sums[2]
                + lax.dot_general(x, wd_ref[:, at], (((1,), (1,)), ((), ())), preferred_element_type=jnp.float32),
            )

        zero = jnp.zeros((plane, hidden), jnp.float32)
        gates, ups, backs = lax.fori_loop(0, PIECES, add, (zero, zero, zero))
        marks = rows_ref[rows, width:].astype(jnp.float32)
        which = lax.broadcasted_iota(jnp.int32, (UNIT, 128), 1)
        gate_parts, up_parts = [], []
        for k in range(PAIR):
            low, high = k * both, k * both + UNIT
            gate_pre, up_pre, back = gates[low:high], ups[low:high], backs[high : high + UNIT]
            sig = jax.nn.sigmoid(gate_pre)
            act = gate_pre * sig
            part = jnp.sum(act * up_pre * back, axis=1, keepdims=True)
            start = pl.multiple_of((z_src * PAIR + k) * message, 8)
            pbuf[pl.ds(start, UNIT), :] = jnp.broadcast_to(part, (UNIT, 128))
            pbuf[pl.ds(start + UNIT, 8), :] = over
            weight = jnp.sum(jnp.where(which == c, marks[low:high], 0.0), axis=1, keepdims=True)
            act_grad = weight * back
            d_gate = act_grad * up_pre * sig * (1.0 + gate_pre * (1.0 - sig))
            d_up = act_grad * act
            gate_parts.append(d_gate)
            up_parts.append(d_up)
        out = pl.ds(pl.multiple_of(z_src * both, 16), both)
        dcat_ref[out, :hidden] = jnp.concatenate(gate_parts, axis=0).astype(jnp.bfloat16)
        dcat_ref[out, hidden:] = jnp.concatenate(up_parts, axis=0).astype(jnp.bfloat16)

    def sums_of(z_to, c_to):
        return pbuf.at[pl.ds(pl.multiple_of((z_to * PAIR + c_to) * message, 8), message), :]

    def sums_from(index):
        return rbuf.at[pl.ds(pl.multiple_of(index * message, 8), message), :]

    def home(z_to, c_to, y_to):
        return remote(
            sums_of(z_to, c_to), sums_from(mine), back_sem.at[z_to, c_to, y_to], home_sem.at[mine],
            {"expert": y_to * PAIR + c_to, "dp": z_to},
        )

    def not_me(z_to, c_to, y_to):
        return (z_to != z) | (c_to != c) | (y_to != y)

    def finish(z_src):
        forward(z_src)
        for c_to in range(PAIR):
            for y_to in range(y_count):

                @pl.when(not_me(z_src, c_to, y_to))
                def _(c_to=c_to, y_to=y_to):
                    home(z_src, c_to, y_to).start()

    def finish_hop(hop):
        if hop == 0:
            finish(z)
            return

        @pl.when(z >= hop)
        def _():
            finish(z - hop)

        @pl.when(z + hop < z_count)
        def _():
            finish(z + hop)

    for load in loads[3:]:
        load.wait()
    for hop in range(1, z_count):
        for p in range(PIECES):

            @pl.when(z >= hop)
            def _(p=p, hop=hop):
                arrived(z - hop, c, p)

                @pl.when(z + 1 < z_count)
                def _():
                    to_up(z - hop, p).start()

                to_core(z - hop, p).start()

            @pl.when(z + hop < z_count)
            def _(p=p, hop=hop):
                arrived(z + hop, c, p)

                @pl.when(z > 0)
                def _():
                    to_down(z + hop, p).start()

                to_core(z + hop, p).start()

            if p == 1:
                finish_hop(hop - 1)
    finish_hop(z_count - 1)

    rbuf[pl.ds(pl.multiple_of(mine * message, 8), message), :] = pbuf[
        pl.ds(pl.multiple_of((z * PAIR + c) * message, 8), message), :
    ]

    for p in range(PIECES):
        across(p).wait_send()
        for z_src in range(z_count):
            to_core(z_src, p).wait_send()

            @pl.when((z_src <= z) & (z + 1 < z_count))
            def _(p=p, z_src=z_src):
                to_up(z_src, p).wait_send()

            @pl.when((z_src >= z) & (z > 0))
            def _(p=p, z_src=z_src):
                to_down(z_src, p).wait_send()

    for z_to in range(z_count):
        for c_to in range(PAIR):
            for y_to in range(y_count):

                @pl.when(not_me(z_to, c_to, y_to))
                def _(z_to=z_to, c_to=c_to, y_to=y_to):
                    home(z_to, c_to, y_to).wait_send()
                    index = (y_to * PAIR + c_to) * z_count + z_to
                    remote(
                        sums_from(index), sums_from(index), load_sem.at[0], home_sem.at[index],
                        {"expert": y * PAIR + 1 - c},
                    ).wait_recv()

    result = jnp.zeros(ids.shape, jnp.float32)
    flags = over
    for e in range(experts):
        sums = jnp.zeros((UNIT, 128), jnp.float32)
        for k in range(z_count):
            first = (e * z_count + k) * message
            sums = sums + rbuf[first : first + UNIT, :]
            flags = jnp.maximum(flags, rbuf[first + UNIT : first + message, :])
        value = jnp.sum(picks[e] * sums, axis=0, keepdims=True)
        result += jnp.where(ids == e, value, 0.0)
    grad_ref[...] = result
    flag_ref[...] = flags


def back_kernel(rows_ref, dcat_ref, gate_ref, up_ref):
    hidden = gate_ref.shape[1]
    both = dot_first(rows_ref[...], dcat_ref[...]).astype(jnp.bfloat16)
    gate_ref[...] = both[:, :hidden]
    up_ref[...] = both[:, hidden:]


def moved(*args):
    tokens, cotangent, route_ids, route_weight, gate_weight, up_weight, down_weight = args
    y_count = lax.axis_size("expert") // PAIR
    z_count = lax.axis_size("dp")
    tok_count, width = tokens.shape
    hidden = gate_weight.shape[2]
    both = 2 * UNIT
    units = PAIR * z_count
    group = units * y_count
    message = UNIT + 8
    dma = pltpu.SemaphoreType.DMA
    rows, dcat, grad, flag = pl.pallas_call(
        functools.partial(move_kernel, z_count),
        out_shape=(
            jax.ShapeDtypeStruct((units * UNIT, width), jnp.bfloat16),
            jax.ShapeDtypeStruct((units * UNIT, 2 * hidden), jnp.bfloat16),
            jax.ShapeDtypeStruct(route_ids.shape[::-1], jnp.float32),
            jax.ShapeDtypeStruct((8, 128), jnp.float32),
        ),
        in_specs=[pl.BlockSpec(memory_space=pltpu.VMEM if i == 1 else pl.ANY) for i in range(7)],
        out_specs=[pl.BlockSpec(memory_space=pltpu.VMEM)] * 4,
        scratch_shapes=[
            pltpu.VMEM((units * both, width + 128), jnp.bfloat16),
            pltpu.VMEM(route_ids.shape[::-1], jnp.int32),
            pltpu.VMEM((tok_count, width), jnp.bfloat16),
            pltpu.VMEM((tok_count, width), jnp.bfloat16),
            pltpu.VMEM((width, hidden), jnp.bfloat16),
            pltpu.VMEM((width, hidden), jnp.bfloat16),
            pltpu.VMEM((hidden, width), jnp.bfloat16),
            pltpu.VMEM((both, width + 128), jnp.bfloat16),
            pltpu.VMEM((both, width + 128), jnp.bfloat16),
            pltpu.VMEM((units * message, 128), jnp.float32),
            pltpu.VMEM((group * message, 128), jnp.float32),
            dma((6,)),
            dma((PIECES,)),
            dma((PIECES,)),
            dma((z_count, PIECES)),
            dma((z_count, PIECES)),
            dma((z_count, PIECES)),
            dma((z_count, PAIR, PIECES)),
            dma((z_count, PAIR, y_count)),
            dma((group,)),
        ],
        compiler_params=pltpu.CompilerParams(
            collective_id=0, has_side_effects=True, vmem_limit_bytes=60 * 2**20
        ),
        cost_estimate=pl.CostEstimate(
            flops=6 * units * both * width * hidden,
            bytes_accessed=8 * width * hidden,
            transcendentals=units * UNIT * hidden,
        ),
    )(
        route_ids.T, route_weight.T, tokens, cotangent,
        gate_weight[0], up_weight[0], down_weight[0],
    )

    def fitting():
        tile = math.gcd(width, 1024)
        gate, up = pl.pallas_call(
            back_kernel,
            out_shape=(jax.ShapeDtypeStruct((width, hidden), jnp.bfloat16),) * 2,
            grid=(width // tile,),
            in_specs=[
                pl.BlockSpec((units * UNIT, tile), lambda i: (0, i)),
                pl.BlockSpec((units * UNIT, 2 * hidden), lambda i: (0, 0)),
            ],
            out_specs=(pl.BlockSpec((tile, hidden), lambda i: (i, 0)),) * 2,
            compiler_params=pltpu.CompilerParams(vmem_limit_bytes=60 * 2**20),
        )(rows, dcat)
        return gate[None], up[None], grad.T

    return lax.cond(flag[0, 0] > 0.5, lambda: general(*args), fitting)


def fits(mesh):
    return mesh.shape["expert"] == 2 * PAIR and mesh.shape["dp"] <= 8


def solution(mesh):
    return jax.shard_map(
        moved if fits(mesh) else general,
        mesh=mesh,
        in_specs=(
            P(("groups", "expert", "dp"), None),
            P(("groups", "expert", "dp"), None),
            P(("groups", "expert", "dp"), None),
            P(("groups", "expert", "dp"), None),
            P("expert", None, "dp"),
            P("expert", None, "dp"),
            P("expert", "dp", None),
        ),
        out_specs=(
            P(("groups", "expert"), None, "dp"),
            P(("groups", "expert"), None, "dp"),
            P(("groups", "expert", "dp"), None),
        ),
        check_vma=False,
    )
```
